512 devices in a mesh: blk: 32 (over z_hi, y, core), amp: 16 (over z_lo, x).
Axes of the slice: x: 4, y: 8, z: 8 (z_hi: 2, z_lo: 4; z = z_hi * 4 + z_lo), core: 2. Of those that a mesh axis runs over, the one named last changes fastest.
Arguments:
- amplitudes: bfloat16 [6144, 163840], P('blk', 'amp'), may hold values from -6 to 6
- integrals: bfloat16 [512, 163840], P('blk', 'amp'), may hold values from -0.02734375 to 0.02734375
- occ_pair: float32 [6144], P('blk'), may hold values from -3 to -0.5
- vir_pair: float32 [512], P('amp'), may hold values from 0.5 to 4
Outputs:
- update: float32 [6144, 512], P('blk', 'amp')
The draws below stay inside these ranges and needn't reach their ends.
All inputs are finite; a program needn't handle non-finite values.
Results may differ from the reference program's by a relative error of at most 0.0003.
Values may be sent and summed in bfloat16 or wider, within the bound.
No kernel may reach another device: no remote copies, remote signals or barrier semaphores. Data moves between devices by JAX's collectives and lax.ppermute only.
A program may use at most 64 MiB of HBM per device.

```python
import jax
import jax.numpy as jnp
from jax import lax

CD = 163840
IJ = 6144
AB = 512


def strengthened(drawn, own_key, source, target, blocks, factor):
    def block_of(position):
        return (jnp.arange(drawn.shape[position]) // (drawn.shape[position] // blocks)).reshape((-1,) + (1,) * (drawn.ndim - 1 - position))

    one_side = jax.random.permutation(own_key, blocks)[block_of(target)]
    other_side = (block_of(target) + blocks // 2) % blocks
    return jnp.where((block_of(source) == one_side) | (block_of(source) == other_side), factor * drawn, drawn)


def levels(stream_key, extent, shards, least, high):
    gain = 1.0
    for dim, blocks in shards:
        heights = jax.random.uniform(jax.random.fold_in(jax.random.fold_in(stream_key, 6), dim), (blocks,), jnp.float32, least / len(shards), high / len(shards))
        gain = gain * jnp.repeat(jnp.exp(heights), extent[dim] // blocks).reshape((-1,) + (1,) * (len(extent) - 1 - dim))
    return gain


def gaussian(own_key, shape, deviation, reach, shards=(), kind=jnp.bfloat16):
    array = jax.random.normal(own_key, shape, jnp.float32) * deviation
    if len(shards) > 0:
        array = levels(own_key, shape, shards, -0.22, 0.18) * array
    return jnp.clip(array, min=-reach, max=reach).astype(kind)


def noise_with(key, extent, scale, bound, cuts, heavy, kind=jnp.bfloat16):
    entries = scale * jax.random.normal(key, extent, jnp.float32)
    if cuts:
        entries = entries * levels(key, extent, cuts, -0.22, 0.18)
    return jnp.clip(strengthened(entries, jax.random.fold_in(key, 3), *heavy), -bound, bound).astype(kind)


def setup_inputs(seed: int = 0) -> dict:
    streams_of = jax.random.split(jax.random.key(seed), 5)
    return {
        "amplitudes": gaussian(streams_of[0], (IJ, CD), 1.0, 6.0, ((0, 32), (1, 16))),
        "integrals": noise_with(streams_of[1], (AB, CD), CD ** -0.5, 0.02734375, ((0, 32), (1, 16)), (1, 0, 32, 2.75)),
        "occ_pair": jnp.clip(-3.0 + 2.5 * jax.random.uniform(streams_of[2], (IJ,), jnp.float32) ** levels(streams_of[2], (IJ,), ((0, 32),), -0.2, 0.2), -3.0, -0.5),
        "vir_pair": jnp.clip(0.5 + 3.5 * jax.random.uniform(streams_of[3], (AB,), jnp.float32) ** levels(streams_of[3], (AB,), ((0, 16),), -0.2, 0.2), 0.5, 4.0),
    }


def reference(amplitudes, integrals, occ_pair, vir_pair):
    residual = lax.dot_general(amplitudes, integrals, (((1,), (1,)), ((), ())), preferred_element_type=jnp.float32)
    return residual / (vir_pair[None, :] - occ_pair[:, None])
```

```python
import functools

import jax
import jax.numpy as jnp
from jax import lax
from jax.experimental import pallas as pl
from jax.experimental.pallas import tpu as pltpu
from jax.sharding import Mesh, PartitionSpec as P

AXES = ("zh", "y", "core", "zl", "x")
STEPS = 5


def product_kernel(keys, ny, mine, other, *refs):
    n = len(keys)
    blocks, out, acc = refs[:n], refs[n], refs[n + 1]
    rows, depth = mine.shape
    height = blocks[0].shape[0]
    kb = depth // STEPS
    for k in range(STEPS):
        cut = slice(k * kb, (k + 1) * kb)
        thin = jnp.concatenate([b[:, cut] for b in blocks], axis=0)
        for side, ref in enumerate((mine, other)):
            part = lax.dot_general(
                ref[:, cut], thin, (((1,), (1,)), ((), ())), preferred_element_type=jnp.float32
            )
            if k == 0:
                acc[side] = part
            else:
                acc[side] += part
    zh, y, core = lax.axis_index("zh"), lax.axis_index("y"), lax.axis_index("core")
    for side in range(2):
        turned = acc[side].T
        for i, (p, s) in enumerate(keys):
            home = lax.rem(zh + p, 2) * ny + lax.rem(y + s + ny, ny)
            slot = lax.rem(core + side, 2) * (2 * ny) + home
            out[pl.ds(slot, 1)] = turned[i * height : (i + 1) * height][None]


def products(keys, ny, mine, other, blocks):
    n = len(blocks)
    rows, depth = mine.shape
    height = blocks[0].shape[0]
    return pl.pallas_call(
        functools.partial(product_kernel, keys, ny),
        in_specs=[pl.BlockSpec(memory_space=pltpu.VMEM)] * (2 + n),
        out_specs=pl.BlockSpec(memory_space=pltpu.VMEM),
        out_shape=jax.ShapeDtypeStruct((2 * n, height, rows), jnp.float32),
        scratch_shapes=[pltpu.VMEM((2, rows, n * height), jnp.float32)],
        compiler_params=pltpu.CompilerParams(vmem_limit_bytes=6 * 1024 * 1024),
        cost_estimate=pl.CostEstimate(
            flops=4 * n * height * rows * depth,
            bytes_accessed=2 * (2 * rows + n * height) * depth,
            transcendentals=0,
        ),
    )(mine, other, *blocks)


def body(sizes, amplitudes, integrals, occ_pair, vir_pair):
    ny = sizes["y"]
    up = [(i, (i + 1) % ny) for i in range(ny)]
    down = [(i, (i - 1) % ny) for i in range(ny)]
    step = {1: down, -1: up}
    swap = [(0, 1), (1, 0)]
    height, rows = integrals.shape[0], amplitudes.shape[0]
    half = ny // 2

    held = {(0, 0): integrals, (1, 0): lax.ppermute(integrals, "zh", swap)}
    for s in range(1, half + 1):
        for p in range(2):
            for d in (1, -1):
                if s < half or d == (1, -1)[p]:
                    held[p, d * s] = lax.ppermute(held[p, d * (s - 1)], "y", step[d])
    other = lax.ppermute(amplitudes, "core", swap)

    keys = list(held)
    sent = products(keys, ny, amplitudes, other, [held[k] for k in keys])
    got = lax.all_to_all(sent, ("core", "zl", "x"), 0, 0, tiled=True)
    total = got.reshape(2, 2 * ny, height, rows).sum(axis=1).reshape(2 * height, rows)
    return (total / (vir_pair[:, None] - occ_pair[None, :])).T


def solution(mesh):
    blk, amp = mesh.shape["blk"], mesh.shape["amp"]
    sizes = {"zh": 2, "y": blk // 4, "core": 2, "zl": 4, "x": amp // 4}
    fine = Mesh(mesh.devices.reshape(tuple(sizes[a] for a in AXES)), AXES)
    b, a = ("zh", "y", "core"), ("zl", "x")
    return jax.shard_map(
        functools.partial(body, sizes),
        mesh=fine,
        in_specs=(P(b, a), P(b, a), P(b), P(a)),
        out_specs=P(b, a),
        check_vma=False,
    )
```

```python
import functools

import jax
import jax.numpy as jnp
from jax import lax
from jax.experimental import pallas as pl
from jax.experimental.pallas import tpu as pltpu
from jax.sharding import Mesh, PartitionSpec as P

AXES = ("zh", "y", "core", "zl", "x")
STEPS = 5
LANES = 128


def product_kernel(keys, ny, mine, other, *refs):
    n = len(keys)
    blocks, out, acc = refs[:n], refs[n], refs[n + 1]
    rows, depth = mine.shape
    height = blocks[0].shape[0]
    kb = depth // STEPS
    for k in range(STEPS):
        cut = slice(k * kb, (k + 1) * kb)
        thin = jnp.concatenate([b[:, cut] for b in blocks], axis=0)
        for side, ref in enumerate((mine, other)):
            part = lax.dot_general(
                ref[:, cut], thin, (((1,), (1,)), ((), ())), preferred_element_type=jnp.float32
            )
            if k == 0:
                acc[side] = part
            else:
                acc[side] += part
    zh, y, core = lax.axis_index("zh"), lax.axis_index("y"), lax.axis_index("core")
    half = height // 2
    for side in range(2):
        turned = acc[side].T
        for i, (p, s) in enumerate(keys):
            home = lax.rem(zh + p, 2) * ny + lax.rem(y + s * (1 - 2 * core) + ny, ny)
            slot = lax.rem(core + side, 2) * (2 * ny) + home
            tile = turned[i * height : (i + 1) * height]
            out[pl.ds(slot, 1), :height] = tile[None, :, :LANES]
            rest = jnp.concatenate([tile[:half, LANES:], tile[half:, LANES:]], axis=1)
            out[pl.ds(slot, 1), height:] = rest[None]


def fetch_kernel(mine, own, mine_near, own_near, sems):
    copies = [
        pltpu.make_async_copy(mine, mine_near, sems.at[0]),
        pltpu.make_async_copy(own, own_near, sems.at[1]),
    ]
    for copy in copies:
        copy.start()
    for copy in copies:
        copy.wait()


def fetch(mine, own):
    return pl.pallas_call(
        fetch_kernel,
        in_specs=[pl.BlockSpec(memory_space=pl.ANY)] * 2,
        out_specs=[pl.BlockSpec(memory_space=pltpu.VMEM)] * 2,
        out_shape=[jax.ShapeDtypeStruct(a.shape, a.dtype) for a in (mine, own)],
        scratch_shapes=[pltpu.SemaphoreType.DMA((2,))],
        compiler_params=pltpu.CompilerParams(vmem_limit_bytes=2 * 1024 * 1024),
        cost_estimate=pl.CostEstimate(
            flops=0, bytes_accessed=4 * (mine.size + own.size), transcendentals=0
        ),
    )(mine, own)


def products(keys, ny, mine, other, blocks):
    n = len(blocks)
    rows, depth = mine.shape
    height = blocks[0].shape[0]
    return pl.pallas_call(
        functools.partial(product_kernel, keys, ny),
        in_specs=[pl.BlockSpec(memory_space=pltpu.VMEM)] * (2 + n),
        out_specs=pl.BlockSpec(memory_space=pltpu.VMEM),
        out_shape=jax.ShapeDtypeStruct((2 * n, height * rows // LANES, LANES), jnp.float32),
        scratch_shapes=[pltpu.VMEM((2, rows, n * height), jnp.float32)],
        compiler_params=pltpu.CompilerParams(vmem_limit_bytes=8 * 1024 * 1024),
        cost_estimate=pl.CostEstimate(
            flops=4 * n * height * rows * depth,
            bytes_accessed=2 * (2 * rows + n * height) * depth,
            transcendentals=0,
        ),
    )(mine, other, *blocks)


def body(sizes, amplitudes, integrals, occ_pair, vir_pair):
    ny = sizes["y"]
    swap = [(0, 1), (1, 0)]
    height, rows = integrals.shape[0], amplitudes.shape[0]
    tie = lax.optimization_barrier

    def hop(block, away):
        pairs = [(2 * i + c, 2 * ((i - away * (1 - 2 * c)) % ny) + c) for i in range(ny) for c in range(2)]
        return lax.ppermute(block, ("y", "core"), pairs)

    near, far = {0: integrals}, {0: lax.ppermute(integrals, "zh", swap)}
    for s in (1, 2, 3):
        near[s], near[-s] = hop(near[s - 1], 1), hop(near[1 - s], -1)
    near[4] = hop(near[3], 1)
    other = lax.ppermute(amplitudes, "core", swap)
    for s in (1, 2):
        far[s], far[-s] = hop(far[s - 1], 1), hop(far[1 - s], -1)
    far[3] = hop(far[2], 1)
    last, near[-3] = tie((far[-2], near[-3]))
    far[-3] = hop(last, -1)
    last, near[4], near[-3] = tie((far[3], near[4], near[-3]))
    far[4] = hop(last, 1)

    held = {(p, s): block for p, plane in enumerate((near, far)) for s, block in plane.items()}
    mine, held[0, 0] = fetch(amplitudes, integrals)
    keys = list(held)
    sent = products(keys, ny, mine, other, [held[k] for k in keys])
    got = lax.all_to_all(sent, ("core", "zl", "x"), 0, 0, tiled=True)
    total = got.reshape(2, 2 * ny, -1, LANES).sum(axis=1)
    left, rest = total[:, :height], total[:, height:]
    right = jnp.concatenate([rest[..., : rows - LANES], rest[..., rows - LANES :]], axis=1)
    total = jnp.concatenate([left, right], axis=2).reshape(2 * height, rows)
    return (total / (vir_pair[:, None] - occ_pair[None, :])).T


def solution(mesh):
    blk, amp = mesh.shape["blk"], mesh.shape["amp"]
    sizes = {"zh": 2, "y": blk // 4, "core": 2, "zl": 4, "x": amp // 4}
    fine = Mesh(mesh.devices.reshape(tuple(sizes[a] for a in AXES)), AXES)
    b, a = ("zh", "y", "core"), ("zl", "x")
    return jax.shard_map(
        functools.partial(body, sizes),
        mesh=fine,
        in_specs=(P(b, a), P(b, a), P(b), P(a)),
        out_specs=P(b, a),
        check_vma=False,
    )
```

```python
import functools

import jax
import jax.numpy as jnp
from jax import lax
from jax.experimental import pallas as pl
from jax.experimental.pallas import tpu as pltpu
from jax.sharding import Mesh, PartitionSpec as P

AXES = ("zh", "y", "core", "zl", "x")
STEPS = 5
LANES = 128


def product_kernel(keys, ny, mark, mine, other, *refs):
    n = len(keys)
    blocks, out, acc = refs[:n], refs[n], refs[n + 1]
    rows, depth = mine.shape
    height = blocks[0].shape[0]
    kb = depth // STEPS
    for k in range(STEPS):
        cut = slice(k * kb, (k + 1) * kb)
        thin = jnp.concatenate([b[:, cut] for b in blocks], axis=0)
        for side, ref in enumerate((mine, other)):
            part = lax.dot_general(
                ref[:, cut], thin, (((1,), (1,)), ((), ())), preferred_element_type=jnp.float32
            )
            if k == 0:
                acc[side] = part
            else:
                acc[side] += part
    zh, y, core = lax.axis_index("zh"), lax.axis_index("y"), lax.axis_index("core")
    half = height // 2
    for side in range(2):
        turned = acc[side].T
        for i, (p, s) in enumerate(keys):
            home = lax.rem(zh + p, 2) * ny + lax.rem(y + s * (1 - 2 * core) + ny, ny)
            slot = lax.rem(core + side, 2) * (2 * ny) + home
            tile = turned[i * height : (i + 1) * height]
            out[pl.ds(slot, 1), :height] = tile[None, :, :LANES]
            rest = jnp.concatenate([tile[:half, LANES:], tile[half:, LANES:]], axis=1)
            out[pl.ds(slot, 1), height:] = rest[None]


def fetch_kernel(mine, own, mine_near, own_near, sems):
    copies = [
        pltpu.make_async_copy(mine, mine_near, sems.at[0]),
        pltpu.make_async_copy(own, own_near, sems.at[1]),
    ]
    for copy in copies:
        copy.start()
    for copy in copies:
        copy.wait()


def fetch(mine, own):
    return pl.pallas_call(
        fetch_kernel,
        in_specs=[pl.BlockSpec(memory_space=pl.ANY)] * 2,
        out_specs=[pl.BlockSpec(memory_space=pltpu.VMEM)] * 2,
        out_shape=[jax.ShapeDtypeStruct(a.shape, a.dtype) for a in (mine, own)],
        scratch_shapes=[pltpu.SemaphoreType.DMA((2,))],
        compiler_params=pltpu.CompilerParams(vmem_limit_bytes=2 * 1024 * 1024),
        cost_estimate=pl.CostEstimate(
            flops=0, bytes_accessed=4 * (mine.size + own.size), transcendentals=0
        ),
    )(mine, own)


def mark_kernel(block, out):
    out[...] = jnp.zeros_like(out)


def mark_after(block):
    return pl.pallas_call(
        mark_kernel,
        in_specs=[pl.BlockSpec(memory_space=pl.ANY)],
        out_specs=pl.BlockSpec(memory_space=pltpu.VMEM),
        out_shape=jax.ShapeDtypeStruct((8, LANES), jnp.int32),
        compiler_params=pltpu.CompilerParams(vmem_limit_bytes=1024 * 1024),
        cost_estimate=pl.CostEstimate(flops=46_000_000_000, bytes_accessed=0, transcendentals=0),
    )(block)


def products(keys, ny, mark, mine, other, blocks):
    n = len(blocks)
    rows, depth = mine.shape
    height = blocks[0].shape[0]
    return pl.pallas_call(
        functools.partial(product_kernel, keys, ny),
        in_specs=[pl.BlockSpec(memory_space=pl.ANY)] + [pl.BlockSpec(memory_space=pltpu.VMEM)] * (2 + n),
        out_specs=pl.BlockSpec(memory_space=pltpu.VMEM),
        out_shape=jax.ShapeDtypeStruct((2 * n, height * rows // LANES, LANES), jnp.float32),
        scratch_shapes=[pltpu.VMEM((2, rows, n * height), jnp.float32)],
        compiler_params=pltpu.CompilerParams(vmem_limit_bytes=8 * 1024 * 1024),
        cost_estimate=pl.CostEstimate(
            flops=4 * n * height * rows * depth,
            bytes_accessed=2 * (2 * rows + n * height) * depth,
            transcendentals=0,
        ),
    )(mark, mine, other, *blocks)


def body(sizes, amplitudes, integrals, occ_pair, vir_pair):
    ny = sizes["y"]
    swap = [(0, 1), (1, 0)]
    height, rows = integrals.shape[0], amplitudes.shape[0]
    tie = lax.optimization_barrier

    def hop(block, away):
        pairs = [(2 * i + c, 2 * ((i - away * (1 - 2 * c)) % ny) + c) for i in range(ny) for c in range(2)]
        return lax.ppermute(block, ("y", "core"), pairs)

    near, far = {0: integrals}, {0: lax.ppermute(integrals, "zh", swap)}
    near[1], near[-1] = hop(near[0], 1), hop(near[0], -1)
    near[2], near[-2] = hop(near[1], 1), hop(near[-1], -1)
    other = lax.ppermute(amplitudes, "core", swap)
    far[0], mark = tie((far[0], mark_after(far[0])))
    far[1] = hop(far[0], 1)
    last, near[2] = tie((far[0], near[2]))
    far[-1] = hop(last, -1)
    near[3], near[-3] = hop(near[2], 1), hop(near[-2], -1)
    last, other = tie((far[1], other))
    far[2] = hop(last, 1)
    far[-2] = hop(far[-1], -1)
    near[4] = hop(near[3], 1)
    last, near[-2] = tie((far[2], near[-2]))
    far[3], far[-3] = hop(last, 1), hop(far[-2], -1)
    far[4] = hop(far[3], 1)

    held = {(p, s): block for p, plane in enumerate((near, far)) for s, block in plane.items()}
    mine, held[0, 0] = fetch(amplitudes, integrals)
    keys = list(held)
    sent = products(keys, ny, mark, mine, other, [held[k] for k in keys])
    got = lax.all_to_all(sent, ("core", "zl", "x"), 0, 0, tiled=True)
    total = got.reshape(2, 2 * ny, -1, LANES).sum(axis=1)
    left, rest = total[:, :height], total[:, height:]
    right = jnp.concatenate([rest[..., : rows - LANES], rest[..., rows - LANES :]], axis=1)
    total = jnp.concatenate([left, right], axis=2).reshape(2 * height, rows)
    return (total / (vir_pair[:, None] - occ_pair[None, :])).T


def solution(mesh):
    blk, amp = mesh.shape["blk"], mesh.shape["amp"]
    sizes = {"zh": 2, "y": blk // 4, "core": 2, "zl": 4, "x": amp // 4}
    fine = Mesh(mesh.devices.reshape(tuple(sizes[a] for a in AXES)), AXES)
    b, a = ("zh", "y", "core"), ("zl", "x")
    return jax.shard_map(
        functools.partial(body, sizes),
        mesh=fine,
        in_specs=(P(b, a), P(b, a), P(b), P(a)),
        out_specs=P(b, a),
        check_vma=False,
    )
```

```python
import functools

import jax
import jax.numpy as jnp
from jax import lax
from jax.experimental import pallas as pl
from jax.experimental.pallas import tpu as pltpu
from jax.sharding import Mesh, PartitionSpec as P

AXES = ("zh", "y", "core", "zl", "x")
STEPS = 5
LANES = 128


def product_kernel(keys, ny, goes_on, before, mine, other, *refs):
    n = len(keys)
    blocks, out, acc = refs[:n], refs[n], refs[n + 1]
    rows, depth = mine.shape
    height = blocks[0].shape[0]
    kb = depth // STEPS
    if goes_on:
        out[...] = before[...]
    for k in range(STEPS):
        cut = slice(k * kb, (k + 1) * kb)
        thin = jnp.concatenate([b[:, cut] for b in blocks], axis=0)
        for side, ref in enumerate((mine, other)):
            part = lax.dot_general(
                ref[:, cut], thin, (((1,), (1,)), ((), ())), preferred_element_type=jnp.float32
            )
            if k == 0:
                acc[side] = part
            else:
                acc[side] += part
    zh, y, core = lax.axis_index("zh"), lax.axis_index("y"), lax.axis_index("core")
    half = height // 2
    for side in range(2):
        turned = acc[side].T
        for i, (p, s) in enumerate(keys):
            home = lax.rem(zh + p, 2) * ny + lax.rem(y + s * (1 - 2 * core) + ny, ny)
            slot = lax.rem(core + side, 2) * (2 * ny) + home
            tile = turned[i * height : (i + 1) * height]
            out[pl.ds(slot, 1), :height] = tile[None, :, :LANES]
            rest = jnp.concatenate([tile[:half, LANES:], tile[half:, LANES:]], axis=1)
            out[pl.ds(slot, 1), height:] = rest[None]


def fetch_kernel(mine, own, mine_near, own_near, sems):
    copies = [
        pltpu.make_async_copy(mine, mine_near, sems.at[0]),
        pltpu.make_async_copy(own, own_near, sems.at[1]),
    ]
    for copy in copies:
        copy.start()
    for copy in copies:
        copy.wait()


def fetch(mine, own):
    return pl.pallas_call(
        fetch_kernel,
        in_specs=[pl.BlockSpec(memory_space=pl.ANY)] * 2,
        out_specs=[pl.BlockSpec(memory_space=pltpu.VMEM)] * 2,
        out_shape=[jax.ShapeDtypeStruct(a.shape, a.dtype) for a in (mine, own)],
        scratch_shapes=[pltpu.SemaphoreType.DMA((2,))],
        compiler_params=pltpu.CompilerParams(vmem_limit_bytes=2 * 1024 * 1024),
        cost_estimate=pl.CostEstimate(
            flops=0, bytes_accessed=4 * (mine.size + own.size), transcendentals=0
        ),
    )(mine, own)


def mark_kernel(block, out):
    out[...] = jnp.zeros_like(out)


def mark_after(block):
    return pl.pallas_call(
        mark_kernel,
        in_specs=[pl.BlockSpec(memory_space=pl.ANY)],
        out_specs=pl.BlockSpec(memory_space=pltpu.VMEM),
        out_shape=jax.ShapeDtypeStruct((8, LANES), jnp.int32),
        compiler_params=pltpu.CompilerParams(vmem_limit_bytes=1024 * 1024),
        cost_estimate=pl.CostEstimate(flops=46_000_000_000, bytes_accessed=0, transcendentals=0),
    )(block)


def products(keys, ny, goes_on, before, mine, other, blocks):
    n = len(blocks)
    rows, depth = mine.shape
    height = blocks[0].shape[0]
    return pl.pallas_call(
        functools.partial(product_kernel, keys, ny, goes_on),
        in_specs=[pl.BlockSpec(memory_space=pltpu.VMEM)] * (3 + n),
        out_specs=pl.BlockSpec(memory_space=pltpu.VMEM),
        out_shape=jax.ShapeDtypeStruct((4 * ny, height * rows // LANES, LANES), jnp.float32),
        scratch_shapes=[pltpu.VMEM((2, rows, n * height), jnp.float32)],
        compiler_params=pltpu.CompilerParams(vmem_limit_bytes=8 * 1024 * 1024),
        cost_estimate=pl.CostEstimate(
            flops=4 * n * height * rows * depth if goes_on else 0,
            bytes_accessed=2 * (2 * rows + n * height) * depth if goes_on else 0,
            transcendentals=0,
        ),
    )(before, mine, other, *blocks)


def body(sizes, amplitudes, integrals, occ_pair, vir_pair):
    ny = sizes["y"]
    swap = [(0, 1), (1, 0)]
    height, rows = integrals.shape[0], amplitudes.shape[0]
    tie = lax.optimization_barrier

    def hop(block, away):
        pairs = [(2 * i + c, 2 * ((i - away * (1 - 2 * c)) % ny) + c) for i in range(ny) for c in range(2)]
        return lax.ppermute(block, ("y", "core"), pairs)

    near, far = {0: integrals}, {0: lax.ppermute(integrals, "zh", swap)}
    near[1], near[-1] = hop(near[0], 1), hop(near[0], -1)
    near[2], near[-2] = hop(near[1], 1), hop(near[-1], -1)
    other = lax.ppermute(amplitudes, "core", swap)
    far[0], mark = tie((far[0], mark_after(far[0])))
    far[1] = hop(far[0], 1)
    last, near[2] = tie((far[0], near[2]))
    far[-1] = hop(last, -1)
    near[3], near[-3] = hop(near[2], 1), hop(near[-2], -1)
    last, other = tie((far[1], other))
    far[2] = hop(last, 1)
    far[-2] = hop(far[-1], -1)
    near[4] = hop(near[3], 1)
    last, near[-2] = tie((far[2], near[-2]))
    far[3], far[-3] = hop(last, 1), hop(far[-2], -1)
    far[4] = hop(far[3], 1)

    held = {(p, s): block for p, plane in enumerate((near, far)) for s, block in plane.items()}
    mine, held[0, 0] = fetch(amplitudes, integrals)
    late = [(0, -3), (0, 4), (1, -3), (1, 4)]
    early = [k for k in held if k not in late]
    sent = products(early, ny, False, mark, mine, other, [held[k] for k in early])
    sent = products(late, ny, True, sent, mine, other, [held[k] for k in late])
    got = lax.all_to_all(sent, ("core", "zl", "x"), 0, 0, tiled=True)
    total = got.reshape(2, 2 * ny, -1, LANES).sum(axis=1)
    left, rest = total[:, :height], total[:, height:]
    right = jnp.concatenate([rest[..., : rows - LANES], rest[..., rows - LANES :]], axis=1)
    total = jnp.concatenate([left, right], axis=2).reshape(2 * height, rows)
    return (total / (vir_pair[:, None] - occ_pair[None, :])).T


def solution(mesh):
    blk, amp = mesh.shape["blk"], mesh.shape["amp"]
    sizes = {"zh": 2, "y": blk // 4, "core": 2, "zl": 4, "x": amp // 4}
    fine = Mesh(mesh.devices.reshape(tuple(sizes[a] for a in AXES)), AXES)
    b, a = ("zh", "y", "core"), ("zl", "x")
    return jax.shard_map(
        functools.partial(body, sizes),
        mesh=fine,
        in_specs=(P(b, a), P(b, a), P(b), P(a)),
        out_specs=P(b, a),
        check_vma=False,
    )
```
